512 devices in a mesh: seq: 64 (over z, y), tensor: 4 (over x), group: 2 (over core).
Axes of the slice: x: 4, y: 4, z: 16, core: 2. Of those that a mesh axis runs over, the one named last changes fastest.
Arguments:
- queries: bfloat16 [32768, 4096], P('seq', ('tensor', 'group')), may hold values from -32 to 32
- cotangent: bfloat16 [32768, 4096], P('seq', ('tensor', 'group')), may hold values from -60 to 60
- encoded: bfloat16 [2, 192, 128, 4096], P(None, 'seq', None, ('tensor', 'group')), may hold values from -16 to 16
- neighbours: int32 [512, 2], P(('seq', 'tensor', 'group')), may hold values from 0 to 191, as said below
Outputs:
- query_grad: bfloat16 [32768, 4096], P('seq', ('tensor', 'group'))
- encoded_grad: bfloat16 [2, 192, 128, 4096], P(None, 'seq', None, ('tensor', 'group'))
The draws below stay inside these ranges and needn't reach their ends.
Inputs may be any that keep to these rules, and one draw needn't show every extreme that they name: `neighbours`: the two ids of a row are different stretches with the same owner id // 3. The 8 rows of index s of seq name each owner o with o // 8 = s // 8 in exactly 1 row, and no other owner. Some stretches are named by many rows.
All inputs are finite; a program needn't handle non-finite values.
Results may differ from the reference program's by a relative error of at most 0.035.
Values may be sent and summed in bfloat16 or wider, within the bound.
A program may use at most 128 MiB of HBM per device.

```python
import math
import jax
import jax.numpy as jnp
from jax import lax

HEADS = 32
HD = 128
STRETCH = 64
R = 128
CH_DEV = 8
NB_DEV = 3
STRETCHES = 512
TOKENS = 32768
NBR = 192
GROUP_SEQ = 8
CAP = 1


def draw_queries(key, part):
    key = jax.random.fold_in(key, 1)
    values = jax.random.truncated_normal(key, -6.0, 6.0, (TOKENS, HEADS * HD), jnp.float32)
    return values.astype(jnp.bfloat16)


def draw_encoded(key, part):
    key = jax.random.fold_in(key, 2)
    first_key = jax.random.fold_in(key, 0)
    values = jax.random.truncated_normal(first_key, -6.0, 6.0, (2, NBR, R, HEADS * HD), jnp.float32)
    return values.astype(jnp.bfloat16)


def draw_cotangent(key, part):
    key = jax.random.fold_in(key, 4)
    keys = jax.random.split(key, 3)
    positions = jnp.arange(TOKENS).astype(jnp.float32)
    trend = jnp.exp(math.log(3.0) * positions / TOKENS)
    row_scale = jnp.exp(jax.random.uniform(keys[1], (TOKENS,), jnp.float32, 0.0, math.log(10.0)))
    column_scale = jnp.exp(jax.random.uniform(keys[2], (HEADS * HD,), jnp.float32, 0.0, math.log(10.0)))
    values = jax.random.truncated_normal(keys[0], -4.0, 4.0, (TOKENS, HEADS * HD), jnp.float32)
    values = values * trend[:, None] * row_scale[:, None] * column_scale[None, :] / 20.0
    return values.astype(jnp.bfloat16)


def draw_neighbours(key, part):
    key = jax.random.fold_in(key, 3)
    keys = jax.random.split(key, 5)
    block_total = STRETCHES // CH_DEV
    block_keys = jax.random.split(keys[0], block_total)

    def block_owners(block_key, index):
        order = jax.random.permutation(block_key, CH_DEV)
        return order // CAP + index // GROUP_SEQ * GROUP_SEQ
    owners = jax.vmap(block_owners)(block_keys, jnp.arange(block_total)).reshape(-1)
    first_draw = jax.random.randint(keys[1], (STRETCHES,), 0, NB_DEV)
    second_draw = jax.random.randint(keys[2], (STRETCHES,), 0, NB_DEV)
    rotation = jax.random.randint(keys[3], (block_total,), 0, NB_DEV)
    popular = (jnp.minimum(first_draw, second_draw) + rotation[owners]) % NB_DEV
    stride = jax.random.randint(keys[4], (STRETCHES,), 1, NB_DEV)
    partner = (popular + stride) % NB_DEV
    return jnp.stack([owners * NB_DEV + popular, owners * NB_DEV + partner], 1).astype(jnp.int32)


def setup_inputs(seed: int = 0) -> dict:
    streams_of = jax.random.split(jax.random.key(seed), 5)
    queries = draw_queries(jax.random.fold_in(streams_of[4], 71), 0)
    cotangent = draw_cotangent(jax.random.fold_in(streams_of[4], 71), 0)
    encoded = draw_encoded(jax.random.fold_in(streams_of[4], 71), 0)
    neighbours = draw_neighbours(jax.random.fold_in(streams_of[4], 71), 0)
    return {"queries": queries, "cotangent": cotangent, "encoded": encoded, "neighbours": neighbours}


def block_grads(query_heads, grad_heads, key_rows, value_rows):
    score_scale = 1.0 / math.sqrt(HD)
    scores = jnp.einsum('gqhd,gkhd->ghqk', query_heads, key_rows) * score_scale
    attention = jax.nn.softmax(scores, axis=-1)
    attention_low = attention.astype(jnp.bfloat16)
    attention_low = lax.optimization_barrier(attention_low).astype(jnp.float32)
    grad_weights = jnp.einsum('gqhd,gkhd->ghqk', grad_heads, value_rows)
    row_delta = lax.optimization_barrier(jnp.sum(attention_low * grad_weights, axis=-1))
    grad_scores = attention * (grad_weights - row_delta[..., None])
    grad_scores_low = grad_scores.astype(jnp.bfloat16)
    grad_scores_low = lax.optimization_barrier(grad_scores_low).astype(jnp.float32)
    query_part = (jnp.einsum('ghqk,gkhd->gqhd', grad_scores_low, key_rows) * score_scale).astype(jnp.bfloat16)
    key_part = jnp.einsum('ghqk,gqhd->gkhd', grad_scores_low, query_heads) * score_scale
    value_part = jnp.einsum('ghqk,gqhd->gkhd', attention_low, grad_heads)
    return (query_part, key_part, value_part)

def reference(queries, cotangent, encoded, neighbours):
    width = HEADS * HD
    query_stretches = queries.reshape(STRETCHES, STRETCH, width)
    grad_stretches = cotangent.reshape(STRETCHES, STRETCH, width)
    zero_stretch = jnp.zeros((1, STRETCH, width), jnp.bfloat16)
    shifted_queries = jnp.concatenate([query_stretches[1:], zero_stretch], 0)
    shifted_grads = jnp.concatenate([grad_stretches[1:], zero_stretch], 0)
    block_size = math.gcd(STRETCHES, 32)
    block_count = STRETCHES // block_size

    def scan_step(running, inputs):
        query_block, grad_block, id_block = inputs
        flat_ids = id_block.reshape(-1).astype(jnp.int32)
        key_rows = encoded[0][flat_ids].astype(jnp.float32).reshape(block_size, 2 * R, HEADS, HD)
        value_rows = encoded[1][flat_ids].astype(jnp.float32).reshape(block_size, 2 * R, HEADS, HD)
        query_heads = query_block.astype(jnp.float32).reshape(block_size, STRETCH, HEADS, HD)
        grad_heads = grad_block.astype(jnp.float32).reshape(block_size, STRETCH, HEADS, HD)
        query_part, key_part, value_part = block_grads(query_heads, grad_heads, key_rows, value_rows)
        running = running.at[0, flat_ids].add(key_part.reshape(block_size * 2, R, width))
        running = running.at[1, flat_ids].add(value_part.reshape(block_size * 2, R, width))
        return (running, query_part.reshape(block_size, STRETCH, width))
    initial = jnp.zeros((2, NBR, R, width), jnp.float32)
    inputs = (shifted_queries.reshape(block_count, block_size, STRETCH, width), shifted_grads.reshape(block_count, block_size, STRETCH, width), neighbours.reshape(block_count, block_size, 2))
    encoded_total, answers = lax.scan(scan_step, initial, inputs)
    answers = answers.reshape(STRETCHES, STRETCH, width)
    query_grad = jnp.concatenate([zero_stretch, answers[:-1]], 0).reshape(TOKENS, width)
    return (query_grad, encoded_total.astype(jnp.bfloat16))
```

```python
import functools
import math

import jax
import jax.numpy as jnp
from jax import lax
from jax.experimental import pallas as pl
from jax.experimental.pallas import tpu as pltpu
from jax.sharding import PartitionSpec as P

HD = 128
GROUP = 8
MESH = pl.DeviceIdType.MESH


def kernel(heads, rows, stored, keys, q_ref, g_ref, e_ref, n_ref, oq_ref, oe_ref, *scratch):
    x = scratch[:heads]
    send = scratch[heads:2 * heads]
    recv = scratch[2 * heads:3 * heads]
    rsend = scratch[3 * heads:4 * heads]
    rrecv = scratch[4 * heads:5 * heads]
    out = scratch[5 * heads:6 * heads]
    (first, enc, egrad, ids, codes, fsem, xsem, esem, isem, osem, gsem, id_send, id_recv, sh_send, sh_recv,
     rq_send, rq_recv, rp_send, rp_recv, bk_send, bk_recv) = scratch[6 * heads:]
    s = lax.axis_index("seq")
    t = lax.axis_index("tensor")
    c = lax.axis_index("group")
    count = lax.axis_size("seq")
    tensors = lax.axis_size("tensor")
    groups = lax.axis_size("group")
    members = tensors * groups
    place = lax.rem(s, GROUP)
    base = s - place
    member = t * groups + c
    has_before, has_after = s > 0, s < count - 1

    def owner_device(k):
        return (base + jnp.bitwise_xor(place, k), t, c)

    def member_device(d):
        other = jnp.bitwise_xor(member, d)
        return (s, other // groups, lax.rem(other, groups))

    barrier = pltpu.get_barrier_semaphore()
    for device in (
        [owner_device(k) for k in range(1, GROUP)]
        + [member_device(d) for d in range(1, members)]
    ):
        pl.semaphore_signal(barrier, inc=1, device_id=device, device_id_type=MESH)

    @pl.when(has_before)
    def _():
        pl.semaphore_signal(barrier, inc=1, device_id=(s - 1, t, c), device_id_type=MESH)

    @pl.when(has_after)
    def _():
        pl.semaphore_signal(barrier, inc=1, device_id=(s + 1, t, c), device_id_type=MESH)

    def columns(h):
        return pl.ds(h * HD, HD)

    id_load = pltpu.make_async_copy(n_ref, ids, isem)
    id_load.start()
    first_loads, x_loads = [], []
    for h in range(heads):
        first_loads.append([
            pltpu.make_async_copy(q_ref.at[0, :, columns(h)], first.at[h, pl.ds(0, rows)], fsem.at[h, 0]),
            pltpu.make_async_copy(g_ref.at[0, :, columns(h)], first.at[h, pl.ds(rows, rows)], fsem.at[h, 1]),
        ])
        for load in first_loads[h]:
            load.start()
    for h in range(heads):
        x_loads.append([
            pltpu.make_async_copy(
                q_ref.at[pl.ds(1, GROUP - 1), :, columns(h)], x[h].at[pl.ds(0, GROUP - 1), pl.ds(0, rows)], xsem.at[h, 0]),
            pltpu.make_async_copy(
                g_ref.at[pl.ds(1, GROUP - 1), :, columns(h)], x[h].at[pl.ds(0, GROUP - 1), pl.ds(rows, rows)], xsem.at[h, 1]),
        ])
        for load in x_loads[h]:
            load.start()
    enc_load = pltpu.make_async_copy(e_ref, enc, esem)
    enc_load.start()

    id_load.wait()
    near, far = ids[0, 0], ids[0, 1]
    owner = near // stored
    excluded = (3 - (near - owner * stored)) - (far - owner * stored)
    codes[member, 0] = lax.rem(owner, GROUP) * 4 + excluded

    with jax.named_scope("barrier"):
        pl.semaphore_wait(barrier, GROUP - 1 + members - 1 + has_before.astype(jnp.int32) + has_after.astype(jnp.int32))

    id_copies = []
    for d in range(1, members):
        copy = pltpu.make_async_remote_copy(
            codes.at[member], codes.at[member], id_send.at[d], id_recv.at[d], device_id=member_device(d), device_id_type=MESH)
        copy.start()
        id_copies.append(copy)
    shifts = []
    for h in range(heads):
        for load in first_loads[h]:
            load.wait()

        copy = pltpu.make_async_remote_copy(
            first.at[h], x[h].at[GROUP - 1], sh_send.at[h], sh_recv.at[h], device_id=(s - 1, t, c), device_id_type=MESH)
        pl.when(has_before)(copy.start)
        shifts.append(copy)

    with jax.named_scope("ids"):
        for copy in id_copies:
            copy.wait_recv()
    code = [codes[j, 0] for j in range(GROUP)]
    slot_of = [jnp.bitwise_xor(code[j] // 4, place) for j in range(GROUP)]
    row_of, left_out = [], []
    for k in range(GROUP):
        row, gone = jnp.int32(0), jnp.int32(0)
        for j in range(GROUP):
            here = slot_of[j] == k
            row = jnp.where(here, jnp.int32(j), row)
            gone = jnp.where(here, lax.rem(code[j], 4), gone)
        row_of.append(row)
        left_out.append(gone)

    both = 2 * rows
    requests = []
    for h in range(heads):
        for load in x_loads[h]:
            load.wait()
        with jax.named_scope("shift"):
            pl.when(has_after)(shifts[h].wait_recv)

        @pl.when(jnp.logical_not(has_after))
        def _():
            x[h][GROUP - 1] = jnp.zeros(x[h].shape[1:], x[h].dtype)

        requests.append([])
        for k in range(GROUP):
            target = recv[h] if k == 0 else send[h]
            target[k, pl.ds(0, both)] = x[h][row_of[k]]
            if h == 0:
                target[k, pl.ds(both, 16)] = jnp.full((16, HD), left_out[k].astype(jnp.float32), jnp.float32).astype(jnp.bfloat16)
            if k:
                copy = pltpu.make_async_remote_copy(
                    send[h].at[k], recv[h].at[k], rq_send.at[h, k], rq_recv.at[h, k],
                    device_id=owner_device(k), device_id_type=MESH)
                copy.start()
                requests[h].append(copy)

    enc_load.wait()
    scale = 1.0 / math.sqrt(HD)
    contract_minor = (((1,), (1,)), ((), ()))
    contract_major = (((0,), (0,)), ((), ()))
    replies, egrad_stores = [], []
    bias = None
    for h in range(heads):
        with jax.named_scope("requests"):
            for copy in requests[h]:
                copy.wait_recv()
        if h == 0:
            lane = lax.broadcasted_iota(jnp.int32, (16, HD), 1)
            parts = []
            for k in range(0, GROUP, 2):
                low = recv[0][k, pl.ds(both, 16)].astype(jnp.float32)
                high = recv[0][k + 1, pl.ds(both, 16)].astype(jnp.float32)
                parts.append(jnp.where(lane < rows, low, high)[0:1])
            gone = jnp.concatenate(parts, axis=1)
            bias = [jnp.where(gone == float(n), jnp.float32(-1e30), jnp.float32(0.0)) for n in range(stored)]
        queries = recv[h][:, pl.ds(0, rows)].reshape(GROUP * rows, HD)
        grads = recv[h][:, pl.ds(rows, rows)].reshape(GROUP * rows, HD)
        key_rows = enc[0, :, :, h * HD:(h + 1) * HD].reshape(stored * keys, HD)
        value_rows = enc[1, :, :, h * HD:(h + 1) * HD].reshape(stored * keys, HD)
        scores = lax.dot_general(key_rows, queries, contract_minor, preferred_element_type=jnp.float32)
        scores = jnp.concatenate([scores[n * keys:(n + 1) * keys] * scale + bias[n] for n in range(stored)], axis=0)
        scores = jnp.exp(scores - jnp.max(scores, axis=0, keepdims=True))
        probs = scores * (1.0 / jnp.sum(scores, axis=0, keepdims=True))
        probs_low = probs.astype(jnp.bfloat16)
        grad_probs = lax.dot_general(value_rows, grads, contract_minor, preferred_element_type=jnp.float32)
        delta = jnp.sum(probs_low.astype(jnp.float32) * grad_probs, axis=0, keepdims=True)
        grad_scores = (probs * (grad_probs - delta)).astype(jnp.bfloat16)
        answer = (lax.dot_general(grad_scores, key_rows, contract_major, preferred_element_type=jnp.float32) * scale)
        answer = answer.astype(jnp.bfloat16).reshape(GROUP, rows, HD)
        rrecv[h][0] = answer[0]
        rsend[h][...] = answer[1:]
        replies.append([])
        for k in range(1, GROUP):
            copy = pltpu.make_async_remote_copy(
                rsend[h].at[k - 1], rrecv[h].at[k], rp_send.at[h, k], rp_recv.at[h, k],
                device_id=owner_device(k), device_id_type=MESH)
            copy.start()
            replies[h].append(copy)
        key_part = lax.dot_general(grad_scores, queries, (((1,), (0,)), ((), ())), preferred_element_type=jnp.float32) * scale
        value_part = lax.dot_general(probs_low, grads, (((1,), (0,)), ((), ())), preferred_element_type=jnp.float32)
        egrad[h, 0] = key_part.astype(jnp.bfloat16).reshape(stored, keys, HD)
        egrad[h, 1] = value_part.astype(jnp.bfloat16).reshape(stored, keys, HD)
        store = pltpu.make_async_copy(egrad.at[h], oe_ref.at[:, :, :, columns(h)], gsem.at[h])
        store.start()
        egrad_stores.append(store)

    backs, out_stores = [], []
    for h in range(heads):
        with jax.named_scope("replies"):
            for copy in replies[h]:
                copy.wait_recv()
        out[h][GROUP - 1] = rrecv[h][slot_of[GROUP - 1]]
        copy = pltpu.make_async_remote_copy(
            out[h].at[GROUP - 1], oq_ref.at[0, :, columns(h)], bk_send.at[h], bk_recv.at[h],
            device_id=(s + 1, t, c), device_id_type=MESH)
        pl.when(has_after)(copy.start)
        backs.append(copy)
        for j in range(GROUP - 1):
            out[h][j] = rrecv[h][slot_of[j]]
        store = pltpu.make_async_copy(
            out[h].at[pl.ds(0, GROUP - 1)], oq_ref.at[pl.ds(1, GROUP - 1), :, columns(h)], osem.at[h])
        store.start()
        out_stores.append(store)

    with jax.named_scope("sends"):
        for copy in id_copies:
            copy.wait_send()
        for h in range(heads):
            pl.when(has_before)(shifts[h].wait_send)
            for copy in requests[h] + replies[h]:
                copy.wait_send()
            egrad_stores[h].wait()

    @pl.when(s == 0)
    def _():
        for h in range(heads):
            first[h] = jnp.zeros(first.shape[1:], first.dtype)
            zero = pltpu.make_async_copy(first.at[h, pl.ds(0, rows)], oq_ref.at[0, :, columns(h)], fsem.at[h, 0])
            zero.start()
            zero.wait()

    with jax.named_scope("stores"):
        for h in range(heads):
            out_stores[h].wait()
            pl.when(has_after)(backs[h].wait_send)
    with jax.named_scope("backs"):
        for h in range(heads):
            pl.when(has_before)(backs[h].wait_recv)


def body(queries, cotangent, encoded, neighbours):
    width = queries.shape[1]
    heads = width // HD
    rows = queries.shape[0] // GROUP
    stored, keys = encoded.shape[1], encoded.shape[2]
    members = lax.axis_size("tensor") * lax.axis_size("group")
    bf16 = jnp.bfloat16
    both = 2 * rows
    dma = pltpu.SemaphoreType.DMA
    scratch = (
        [pltpu.VMEM((GROUP, both, HD), bf16) for _ in range(heads)]
        + [pltpu.VMEM((GROUP, both + (16 if h == 0 else 0), HD), bf16) for h in range(heads)]
        + [pltpu.VMEM((GROUP, both + (16 if h == 0 else 0), HD), bf16) for h in range(heads)]
        + [pltpu.VMEM((GROUP - 1, rows, HD), bf16) for _ in range(heads)]
        + [pltpu.VMEM((GROUP, rows, HD), bf16) for _ in range(heads)]
        + [pltpu.VMEM((GROUP, rows, HD), bf16) for _ in range(heads)]
        + [
            pltpu.VMEM((heads, both, HD), bf16),
            pltpu.VMEM(encoded.shape, bf16),
            pltpu.VMEM((heads, 2, stored, keys, HD), bf16),
            pltpu.SMEM((1, 2), jnp.int32),
            pltpu.SMEM((GROUP, 128), jnp.int32),
            dma((heads, 2)), dma((heads, 2)), dma, dma, dma((heads,)), dma((heads,)),
            dma((members,)), dma((members,)), dma((heads,)), dma((heads,)),
            dma((heads, GROUP)), dma((heads, GROUP)), dma((heads, GROUP)), dma((heads, GROUP)),
            dma((heads,)), dma((heads,)),
        ]
    )
    hbm = pl.BlockSpec(memory_space=pltpu.HBM)
    anywhere = pl.BlockSpec(memory_space=pl.ANY)
    query_grad, encoded_grad = pl.pallas_call(
        functools.partial(kernel, heads, rows, stored, keys),
        out_shape=(
            jax.ShapeDtypeStruct((GROUP, rows, width), bf16),
            jax.ShapeDtypeStruct(encoded.shape, bf16),
        ),
        in_specs=[hbm] * 4,
        out_specs=(anywhere, anywhere),
        scratch_shapes=scratch,
        compiler_params=pltpu.CompilerParams(
            collective_id=0, has_side_effects=True, vmem_limit_bytes=48 * 2**20
        ),
        cost_estimate=pl.CostEstimate(flops=10**9, bytes_accessed=3 * 2**20, transcendentals=10**6),
        name="retrieval_grads",
    )(*[
        pltpu.with_memory_space_constraint(operand, pltpu.HBM)
        for operand in (queries.reshape(GROUP, rows, width), cotangent.reshape(GROUP, rows, width), encoded, neighbours)
    ])
    return query_grad.reshape(queries.shape), encoded_grad


def solution(mesh):
    placed = (
        P("seq", ("tensor", "group")),
        P("seq", ("tensor", "group")),
        P(None, "seq", None, ("tensor", "group")),
        P(("seq", "tensor", "group"), None),
    )
    return jax.shard_map(
        body,
        mesh=mesh,
        in_specs=placed,
        out_specs=(P("seq", ("tensor", "group")), P(None, "seq", None, ("tensor", "group"))),
        check_vma=False,
    )
```

```python
import functools
import math

import jax
import jax.numpy as jnp
from jax import lax
from jax.experimental import pallas as pl
from jax.experimental.pallas import tpu as pltpu
from jax.sharding import PartitionSpec as P

HD = 128
GROUP = 8
SLOTS = (7, 6, 5, 4, 3, 2, 1)
MESH = pl.DeviceIdType.MESH


def kernel(heads, rows, stored, keys, q_ref, g_ref, e_ref, n_ref, oq_ref, oe_ref, *scratch):
    x = scratch[:heads]
    rrecv = scratch[heads:2 * heads]
    out = scratch[2 * heads:3 * heads]
    (send, recv, rsend, first, enc, egrad, low_probs, low_grads, turned, tiles, gone_tiles, bias, ids, codes, fsem, xsem, esem,
     isem, osem, gsem, id_send, id_recv, tl_send, tl_recv, sh_send, sh_recv, rq_send, rq_recv, rp_send, rp_recv, bk_send,
     bk_recv, ready) = scratch[3 * heads:]
    both = 2 * rows
    width = 2 * rows
    pairs = GROUP // 2
    s = lax.axis_index("seq")
    t = lax.axis_index("tensor")
    c = lax.axis_index("group")
    count = lax.axis_size("seq")
    tensors = lax.axis_size("tensor")
    groups = lax.axis_size("group")
    members = tensors * groups
    place = lax.rem(s, GROUP)
    base = s - place
    member = t * groups + c
    has_before, has_after = s > 0, s < count - 1

    def owner_device(k):
        return (base + jnp.bitwise_xor(place, k), t, c)

    def member_device(d):
        other = jnp.bitwise_xor(member, d)
        return (s, other // groups, lax.rem(other, groups))

    barrier = pltpu.get_barrier_semaphore()
    for d in range(1, members):
        pl.semaphore_signal(barrier, inc=1, device_id=member_device(d), device_id_type=MESH)

    @pl.when(jnp.logical_and(has_before, place != 1))
    def _():
        pl.semaphore_signal(barrier, inc=1, device_id=(s - 1, t, c), device_id_type=MESH)

    @pl.when(has_after)
    def _():
        pl.semaphore_signal(barrier, inc=1, device_id=(s + 1, t, c), device_id_type=MESH)

    for k in SLOTS:

        @pl.when(place != k)
        def _():
            pl.semaphore_signal(barrier, inc=1, device_id=owner_device(k), device_id_type=MESH)

    def columns(h):
        return pl.ds(h * HD, HD)

    id_load = pltpu.make_async_copy(n_ref, ids, isem)
    id_load.start()
    first_loads, x_loads, enc_loads = [], [], []
    for h in range(heads):
        first_loads.append([
            pltpu.make_async_copy(ref.at[0, :, columns(h)], first.at[h, pl.ds(half * rows, rows)], fsem.at[h, half])
            for half, ref in enumerate((q_ref, g_ref))
        ])
        for load in first_loads[h]:
            load.start()
    for h in range(heads):
        enc_loads.append(pltpu.make_async_copy(e_ref.at[:, :, :, columns(h)], enc.at[h], esem.at[h]))
        enc_loads[h].start()
    for h in range(heads):
        x_loads.append([
            pltpu.make_async_copy(
                ref.at[pl.ds(1, GROUP - 1), :, columns(h)],
                x[h].at[pl.ds(0, GROUP - 1), pl.ds(half * rows, rows)], xsem.at[h, half])
            for half, ref in enumerate((q_ref, g_ref))
        ])
        for load in x_loads[h]:
            load.start()

    id_load.wait()
    near, far = ids[0, 0], ids[0, 1]
    owner = near // stored
    excluded = (3 - (near - owner * stored)) - (far - owner * stored)
    codes[member, 0] = lax.rem(owner, GROUP) * 4 + excluded

    mates = jnp.where(place == 0, 0, GROUP - 1 + has_after.astype(jnp.int32))
    pl.semaphore_wait(barrier, members - 1 + has_before.astype(jnp.int32) + mates)

    @pl.when(place != 0)
    def _():
        pl.semaphore_signal(ready, inc=1, device_id=(base, t, c), device_id_type=MESH)

    id_copies = []
    for d in range(1, members):
        copy = pltpu.make_async_remote_copy(
            codes.at[member], codes.at[member], id_send.at[d], id_recv.at[d], device_id=member_device(d), device_id_type=MESH)
        copy.start()
        id_copies.append(copy)
    shifts = []
    for h in range(heads):
        for load in first_loads[h]:
            load.wait()
        copy = pltpu.make_async_remote_copy(
            first.at[h], x[h].at[GROUP - 1], sh_send.at[h], sh_recv.at[h], device_id=(s - 1, t, c), device_id_type=MESH)
        pl.when(has_before)(copy.start)
        shifts.append(copy)

    for load in enc_loads:
        load.wait()

    @pl.loop(0, heads)
    def _(h):
        turned[h] = enc[h, 0].reshape(stored * keys, HD).T

    for copy in id_copies:
        copy.wait_recv()
    code = [codes[j, 0] for j in range(GROUP)]
    slot_of = [jnp.bitwise_xor(code[j] // 4, place) for j in range(GROUP)]
    row_of, left_out = [], []
    for k in range(GROUP):
        row, gone = jnp.int32(0), jnp.int32(0)
        for j in range(GROUP):
            here = slot_of[j] == k
            row = jnp.where(here, jnp.int32(j), row)
            gone = jnp.where(here, lax.rem(code[j], 4), gone)
        row_of.append(row)
        left_out.append(gone)

    def tile_copy(k):
        return pltpu.make_async_remote_copy(
            tiles.at[k], gone_tiles.at[k], tl_send.at[k], tl_recv.at[k], device_id=owner_device(k), device_id_type=MESH)

    def request(h, k):
        return pltpu.make_async_remote_copy(
            send.at[h, k], recv.at[h, k], rq_send.at[h, k], rq_recv.at[h, k], device_id=owner_device(k), device_id_type=MESH)

    def reply(h, k, target):
        return pltpu.make_async_remote_copy(
            rsend.at[h, k], target.at[k], rp_send.at[h, k], rp_recv.at[h, k], device_id=owner_device(k), device_id_type=MESH)

    def egrad_store(h):
        start = h * HD if isinstance(h, int) else pl.multiple_of(h * HD, HD)
        return pltpu.make_async_copy(egrad.at[h], oe_ref.at[:, :, :, pl.ds(start, HD)], gsem.at[h])

    @pl.when(place == 0)
    def _():
        pl.semaphore_wait(ready, GROUP - 1)

    for k in SLOTS:
        tiles[k] = jnp.full(tiles.shape[1:], left_out[k].astype(jnp.float32), jnp.float32)
        tile_copy(k).start()
    gone_tiles[0] = jnp.full(tiles.shape[1:], left_out[0].astype(jnp.float32), jnp.float32)
    for h in range(heads):
        for load in x_loads[h]:
            load.wait()
        pl.when(has_after)(shifts[h].wait_recv)

        @pl.when(jnp.logical_not(has_after))
        def _():
            x[h][GROUP - 1] = jnp.zeros(x[h].shape[1:], x[h].dtype)

        for k in SLOTS:
            send[h, k] = x[h][row_of[k]]
            request(h, k).start()
        recv[h, 0] = x[h][row_of[0]]

    scale = 1.0 / math.sqrt(HD)
    minor = (((1,), (1,)), ((), ()))
    plain = (((1,), (0,)), ((), ()))
    lane = lax.broadcasted_iota(jnp.int32, tiles.shape[1:], 1)
    for k in SLOTS:
        tile_copy(k).wait_recv()
    for p in range(pairs):
        gone = jnp.where(lane < rows, gone_tiles[2 * p], gone_tiles[2 * p + 1])
        for m in range(stored):
            bias[p, m] = jnp.where(gone == float(m), jnp.float32(-1e30), jnp.float32(0.0))

    blocks = 2
    span = GROUP // blocks

    @pl.loop(0, heads * blocks)
    def _(step):
        h = step // blocks if blocks > 1 else step
        p = blocks - 1 - lax.rem(step, blocks) if blocks > 1 else 0
        k = span * p
        for i in range(span - 1, -1, -1):
            if i:
                request(h, k + i).wait_recv()
            elif blocks > 1:

                @pl.when(k > 0)
                def _():
                    request(h, k).wait_recv()

        queries = recv[h, pl.ds(k, span), pl.ds(0, rows)].reshape(span * rows, HD)
        grads = recv[h, pl.ds(k, span), pl.ds(rows, rows)].reshape(span * rows, HD)
        key_rows = enc[h, 0].reshape(stored * keys, HD)
        value_rows = enc[h, 1].reshape(stored * keys, HD)
        scores = lax.dot_general(key_rows, queries, minor, preferred_element_type=jnp.float32)
        grad_probs = lax.dot_general(value_rows, grads, minor, preferred_element_type=jnp.float32)
        masks = [jnp.concatenate([bias[p * (span // 2) + i, m][0:1] for i in range(span // 2)], axis=1) for m in range(stored)]
        scores = jnp.concatenate([scores[m * keys:(m + 1) * keys] * scale + masks[m] for m in range(stored)], axis=0)
        scores = jnp.exp(scores - jnp.max(scores, axis=0, keepdims=True))
        probs = scores * (1.0 / jnp.sum(scores, axis=0, keepdims=True))
        probs_low = probs.astype(jnp.bfloat16)
        delta = jnp.sum(probs_low.astype(jnp.float32) * grad_probs, axis=0, keepdims=True)
        grad_scores = (probs * (grad_probs - delta)).astype(jnp.bfloat16)
        low_probs[p] = probs_low
        low_grads[p] = grad_scores
        answer = lax.dot_general(turned[h], grad_scores, plain, preferred_element_type=jnp.float32) * scale
        rsend[h, pl.ds(k, span)] = answer.T.astype(jnp.bfloat16).reshape(span, rows, HD)
        for g in range(heads):

            @pl.when(h == g)
            def _():
                for i in range(span - 1, 0, -1):
                    reply(g, k + i, rrecv[g]).start()

                @pl.when(k > 0)
                def _():
                    reply(g, k, rrecv[g]).start()

                @pl.when(k == 0)
                def _():
                    rrecv[g][0] = rsend[g, 0]

        @pl.when(jnp.int32(k) == 0)
        def _():
            queries = recv[h, :, pl.ds(0, rows)].reshape(GROUP * rows, HD)
            grads = recv[h, :, pl.ds(rows, rows)].reshape(GROUP * rows, HD)
            score_parts = jnp.concatenate([low_grads[i] for i in range(blocks)], axis=1)
            prob_parts = jnp.concatenate([low_probs[i] for i in range(blocks)], axis=1)
            key_part = lax.dot_general(score_parts, queries, plain, preferred_element_type=jnp.float32) * scale
            value_part = lax.dot_general(prob_parts, grads, plain, preferred_element_type=jnp.float32)
            egrad[h, 0] = key_part.astype(jnp.bfloat16).reshape(stored, keys, HD)
            egrad[h, 1] = value_part.astype(jnp.bfloat16).reshape(stored, keys, HD)
            egrad_store(h).start()

    backs, out_stores = [], []
    for h in range(heads):
        for k in SLOTS:
            reply(h, k, rrecv[h]).wait_recv()
        out[h][GROUP - 1] = rrecv[h][slot_of[GROUP - 1]]
        copy = pltpu.make_async_remote_copy(
            out[h].at[GROUP - 1], oq_ref.at[0, :, columns(h)], bk_send.at[h], bk_recv.at[h],
            device_id=(s + 1, t, c), device_id_type=MESH)
        pl.when(has_after)(copy.start)
        backs.append(copy)
        for j in range(GROUP - 1):
            out[h][j] = rrecv[h][slot_of[j]]
        store = pltpu.make_async_copy(
            out[h].at[pl.ds(0, GROUP - 1)], oq_ref.at[pl.ds(1, GROUP - 1), :, columns(h)], osem.at[h])
        store.start()
        out_stores.append(store)

    for copy in id_copies:
        copy.wait_send()
    for k in SLOTS:
        tile_copy(k).wait_send()
    for h in range(heads):
        pl.when(has_before)(shifts[h].wait_send)
        for k in SLOTS:
            request(h, k).wait_send()
            reply(h, k, rrecv[h]).wait_send()
        egrad_store(h).wait()

    @pl.when(jnp.logical_not(has_before))
    def _():
        for h in range(heads):
            first[h] = jnp.zeros(first.shape[1:], first.dtype)
            zero = pltpu.make_async_copy(first.at[h, pl.ds(0, rows)], oq_ref.at[0, :, columns(h)], fsem.at[h, 0])
            zero.start()
            zero.wait()

    for h in range(heads):
        out_stores[h].wait()
        pl.when(has_after)(backs[h].wait_send)
    for h in range(heads):
        pl.when(has_before)(backs[h].wait_recv)


def finish(q_in, e_in, q_out, e_out, sems):
    copies = []
    for i, (source, target) in enumerate(((q_in, q_out), (e_in.at[0], e_out.at[0]), (e_in.at[1], e_out.at[1]))):
        copy = pltpu.make_async_copy(source, target, sems.at[i])
        copy.start()
        copies.append(copy)
    for copy in copies:
        copy.wait()


def body(queries, cotangent, encoded, neighbours):
    width = queries.shape[1]
    heads = width // HD
    rows = queries.shape[0] // GROUP
    stored, keys = encoded.shape[1], encoded.shape[2]
    members = lax.axis_size("tensor") * lax.axis_size("group")
    bf16 = jnp.bfloat16
    both = 2 * rows
    dma = pltpu.SemaphoreType.DMA
    scratch = (
        [pltpu.VMEM((GROUP, both, HD), bf16) for _ in range(heads)]
        + [pltpu.VMEM((GROUP, rows, HD), bf16) for _ in range(2 * heads)]
        + [
            pltpu.VMEM((heads, GROUP, both, HD), bf16),
            pltpu.VMEM((heads, GROUP, both, HD), bf16),
            pltpu.VMEM((heads, GROUP, rows, HD), bf16),
            pltpu.VMEM((heads, both, HD), bf16),
            pltpu.VMEM((heads, 2, stored, keys, HD), bf16),
            pltpu.VMEM((heads, 2, stored, keys, HD), bf16),
            pltpu.VMEM((2, stored * keys, GROUP // 2 * rows), bf16),
            pltpu.VMEM((2, stored * keys, GROUP // 2 * rows), bf16),
            pltpu.VMEM((heads, HD, stored * keys), bf16),
            pltpu.VMEM((GROUP, 8, HD), jnp.float32),
            pltpu.VMEM((GROUP, 8, HD), jnp.float32),
            pltpu.VMEM((GROUP // 2, stored, 8, HD), jnp.float32),
            pltpu.SMEM((1, 2), jnp.int32),
            pltpu.SMEM((GROUP, 128), jnp.int32),
            dma((heads, 2)), dma((heads, 2)), dma((heads,)), dma, dma((heads,)), dma((heads,)),
            dma((members,)), dma((members,)), dma((GROUP,)), dma((GROUP,)), dma((heads,)), dma((heads,)),
            dma((heads, GROUP)), dma((heads, GROUP)), dma((heads, GROUP)), dma((heads, GROUP)),
            dma((heads,)), dma((heads,)), pltpu.SemaphoreType.REGULAR,
        ]
    )
    hbm = pl.BlockSpec(memory_space=pltpu.HBM)
    anywhere = pl.BlockSpec(memory_space=pl.ANY)
    query_grad, encoded_grad = pl.pallas_call(
        functools.partial(kernel, heads, rows, stored, keys),
        out_shape=(
            jax.ShapeDtypeStruct((GROUP, rows, width), bf16),
            jax.ShapeDtypeStruct(encoded.shape, bf16),
        ),
        in_specs=[hbm] * 4,
        out_specs=(anywhere, anywhere),
        scratch_shapes=scratch,
        compiler_params=pltpu.CompilerParams(
            collective_id=0, has_side_effects=True, vmem_limit_bytes=48 * 2**20
        ),
        cost_estimate=pl.CostEstimate(flops=10**9, bytes_accessed=3 * 2**20, transcendentals=10**6),
        name="retrieval_grads",
    )(*[
        pltpu.with_memory_space_constraint(operand, pltpu.HBM)
        for operand in (queries.reshape(GROUP, rows, width), cotangent.reshape(GROUP, rows, width), encoded, neighbours)
    ])
    query_grad, encoded_grad = pl.pallas_call(
        finish,
        out_shape=(
            pltpu.HBM((GROUP, rows, width), bf16),
            pltpu.HBM(encoded.shape, bf16),
        ),
        in_specs=[anywhere] * 2,
        out_specs=(anywhere, anywhere),
        scratch_shapes=[dma((3,))],
        compiler_params=pltpu.CompilerParams(vmem_limit_bytes=2**20),
        cost_estimate=pl.CostEstimate(flops=0, bytes_accessed=3 * 2**20, transcendentals=0),
        name="retrieval_finish",
    )(query_grad, encoded_grad)
    return query_grad.reshape(queries.shape), encoded_grad


def solution(mesh):
    placed = (
        P("seq", ("tensor", "group")),
        P("seq", ("tensor", "group")),
        P(None, "seq", None, ("tensor", "group")),
        P(("seq", "tensor", "group"), None),
    )
    return jax.shard_map(
        body,
        mesh=mesh,
        in_specs=placed,
        out_specs=(P("seq", ("tensor", "group")), P(None, "seq", None, ("tensor", "group"))),
        check_vma=False,
    )
```

```python
import functools
import math

import jax
import jax.numpy as jnp
from jax import lax
from jax.experimental import pallas as pl
from jax.experimental.pallas import tpu as pltpu
from jax.sharding import PartitionSpec as P

HD = 128
GROUP = 8
SLOTS = (6, 7, 5, 4, 2, 3, 1)
MESH = pl.DeviceIdType.MESH


def kernel(heads, rows, stored, keys, q_ref, g_ref, e_ref, n_ref, oq_ref, oe_ref, *scratch):
    x = scratch[:heads]
    rrecv = scratch[heads:2 * heads]
    out = scratch[2 * heads:3 * heads]
    (send, recv, rsend, first, enc, egrad, low_probs, low_grads, turned, tiles, gone_tiles, bias, ids, codes, fsem, xsem, esem,
     isem, osem, gsem, id_send, id_recv, tl_send, tl_recv, sh_send, sh_recv, rq_send, rq_recv, rp_send, rp_recv, bk_send,
     bk_recv, ready) = scratch[3 * heads:]
    both = 2 * rows
    width = 2 * rows
    pairs = GROUP // 2
    s = lax.axis_index("seq")
    t = lax.axis_index("tensor")
    c = lax.axis_index("group")
    count = lax.axis_size("seq")
    tensors = lax.axis_size("tensor")
    groups = lax.axis_size("group")
    members = tensors * groups
    place = lax.rem(s, GROUP)
    base = s - place
    member = t * groups + c
    has_before, has_after = s > 0, s < count - 1

    def owner_device(k):
        return (base + jnp.bitwise_xor(place, k), t, c)

    def member_device(d):
        other = jnp.bitwise_xor(member, d)
        return (s, other // groups, lax.rem(other, groups))

    barrier = pltpu.get_barrier_semaphore()
    for d in range(1, members):
        pl.semaphore_signal(barrier, inc=1, device_id=member_device(d), device_id_type=MESH)

    @pl.when(jnp.logical_and(has_before, place != 1))
    def _():
        pl.semaphore_signal(barrier, inc=1, device_id=(s - 1, t, c), device_id_type=MESH)

    @pl.when(has_after)
    def _():
        pl.semaphore_signal(barrier, inc=1, device_id=(s + 1, t, c), device_id_type=MESH)

    for k in SLOTS:

        @pl.when(place != k)
        def _():
            pl.semaphore_signal(barrier, inc=1, device_id=owner_device(k), device_id_type=MESH)

    def columns(h):
        return pl.ds(h * HD, HD)

    id_load = pltpu.make_async_copy(n_ref, ids, isem)
    id_load.start()
    first_loads, x_loads, enc_loads = [], [], []
    for h in range(heads):
        first_loads.append([
            pltpu.make_async_copy(ref.at[0, :, columns(h)], first.at[h, pl.ds(half * rows, rows)], fsem.at[h, half])
            for half, ref in enumerate((q_ref, g_ref))
        ])
        for load in first_loads[h]:
            load.start()
    for h in range(heads):
        enc_loads.append(pltpu.make_async_copy(e_ref.at[:, :, :, columns(h)], enc.at[h], esem.at[h]))
        enc_loads[h].start()
    for h in range(heads):
        x_loads.append([
            pltpu.make_async_copy(
                ref.at[pl.ds(1, GROUP - 1), :, columns(h)],
                x[h].at[pl.ds(0, GROUP - 1), pl.ds(half * rows, rows)], xsem.at[h, half])
            for half, ref in enumerate((q_ref, g_ref))
        ])
        for load in x_loads[h]:
            load.start()

    id_load.wait()
    near, far = ids[0, 0], ids[0, 1]
    owner = near // stored
    excluded = (3 - (near - owner * stored)) - (far - owner * stored)
    codes[member, 0] = lax.rem(owner, GROUP) * 4 + excluded

    mates = jnp.where(place == 0, 0, GROUP - 1 + has_after.astype(jnp.int32))
    pl.semaphore_wait(barrier, members - 1 + has_before.astype(jnp.int32) + mates)

    @pl.when(place != 0)
    def _():
        pl.semaphore_signal(ready, inc=1, device_id=(base, t, c), device_id_type=MESH)

    id_copies = []
    for d in range(1, members):
        copy = pltpu.make_async_remote_copy(
            codes.at[member], codes.at[member], id_send.at[d], id_recv.at[d], device_id=member_device(d), device_id_type=MESH)
        copy.start()
        id_copies.append(copy)
    shifts = []
    for h in range(heads):
        for load in first_loads[h]:
            load.wait()
        copy = pltpu.make_async_remote_copy(
            first.at[h], x[h].at[GROUP - 1], sh_send.at[h], sh_recv.at[h], device_id=(s - 1, t, c), device_id_type=MESH)
        pl.when(has_before)(copy.start)
        shifts.append(copy)

    for load in enc_loads:
        load.wait()

    @pl.loop(0, heads)
    def _(h):
        turned[h] = enc[h, 0].reshape(stored * keys, HD).T

    for copy in id_copies:
        copy.wait_recv()
    code = [codes[j, 0] for j in range(GROUP)]
    slot_of = [jnp.bitwise_xor(code[j] // 4, place) for j in range(GROUP)]
    row_of, left_out = [], []
    for k in range(GROUP):
        row, gone = jnp.int32(0), jnp.int32(0)
        for j in range(GROUP):
            here = slot_of[j] == k
            row = jnp.where(here, jnp.int32(j), row)
            gone = jnp.where(here, lax.rem(code[j], 4), gone)
        row_of.append(row)
        left_out.append(gone)

    def tile_copy(k):
        return pltpu.make_async_remote_copy(
            tiles.at[k], gone_tiles.at[k], tl_send.at[k], tl_recv.at[k], device_id=owner_device(k), device_id_type=MESH)

    def request(h, k):
        return pltpu.make_async_remote_copy(
            send.at[h, k], recv.at[h, k], rq_send.at[h, k], rq_recv.at[h, k], device_id=owner_device(k), device_id_type=MESH)

    def reply(h, k, target):
        return pltpu.make_async_remote_copy(
            rsend.at[h, k], target.at[k], rp_send.at[h, k], rp_recv.at[h, k], device_id=owner_device(k), device_id_type=MESH)

    def egrad_store(h):
        start = h * HD if isinstance(h, int) else pl.multiple_of(h * HD, HD)
        return pltpu.make_async_copy(egrad.at[h], oe_ref.at[:, :, :, pl.ds(start, HD)], gsem.at[h])

    @pl.when(place == 0)
    def _():
        pl.semaphore_wait(ready, GROUP - 1)

    for k in SLOTS:
        tiles[k] = jnp.full(tiles.shape[1:], left_out[k].astype(jnp.float32), jnp.float32)
        tile_copy(k).start()
    gone_tiles[0] = jnp.full(tiles.shape[1:], left_out[0].astype(jnp.float32), jnp.float32)
    for h in range(heads):
        for load in x_loads[h]:
            load.wait()
        pl.when(has_after)(shifts[h].wait_recv)

        @pl.when(jnp.logical_not(has_after))
        def _():
            x[h][GROUP - 1] = jnp.zeros(x[h].shape[1:], x[h].dtype)

        for k in SLOTS:
            send[h, k] = x[h][row_of[k]]
            request(h, k).start()
        recv[h, 0] = x[h][row_of[0]]

    scale = 1.0 / math.sqrt(HD)
    minor = (((1,), (1,)), ((), ()))
    plain = (((1,), (0,)), ((), ()))
    lane = lax.broadcasted_iota(jnp.int32, tiles.shape[1:], 1)
    for k in SLOTS:
        tile_copy(k).wait_recv()
    for p in range(pairs):
        gone = jnp.where(lane < rows, gone_tiles[2 * p], gone_tiles[2 * p + 1])
        for m in range(stored):
            bias[p, m] = jnp.where(gone == float(m), jnp.float32(-1e30), jnp.float32(0.0))

    blocks = 2
    span = GROUP // blocks

    @pl.loop(0, heads * blocks)
    def _(step):
        h = step // blocks if blocks > 1 else step
        p = blocks - 1 - lax.rem(step, blocks) if blocks > 1 else 0
        k = span * p
        for i in range(span - 1, -1, -1):
            if i:
                request(h, k + i).wait_recv()
            elif blocks > 1:

                @pl.when(k > 0)
                def _():
                    request(h, k).wait_recv()

        queries = recv[h, pl.ds(k, span), pl.ds(0, rows)].reshape(span * rows, HD)
        grads = recv[h, pl.ds(k, span), pl.ds(rows, rows)].reshape(span * rows, HD)
        key_rows = enc[h, 0].reshape(stored * keys, HD)
        value_rows = enc[h, 1].reshape(stored * keys, HD)
        scores = lax.dot_general(key_rows, queries, minor, preferred_element_type=jnp.float32)
        grad_probs = lax.dot_general(value_rows, grads, minor, preferred_element_type=jnp.float32)
        masks = [jnp.concatenate([bias[p * (span // 2) + i, m][0:1] for i in range(span // 2)], axis=1) for m in range(stored)]
        scores = jnp.concatenate([scores[m * keys:(m + 1) * keys] * scale + masks[m] for m in range(stored)], axis=0)
        scores = jnp.exp(scores - jnp.max(scores, axis=0, keepdims=True))
        probs = scores * (1.0 / jnp.sum(scores, axis=0, keepdims=True))
        probs_low = probs.astype(jnp.bfloat16)
        delta = jnp.sum(probs_low.astype(jnp.float32) * grad_probs, axis=0, keepdims=True)
        grad_scores = (probs * (grad_probs - delta)).astype(jnp.bfloat16)
        low_probs[p] = probs_low
        low_grads[p] = grad_scores
        answer = lax.dot_general(turned[h], grad_scores, plain, preferred_element_type=jnp.float32) * scale
        rsend[h, pl.ds(k, span)] = answer.T.astype(jnp.bfloat16).reshape(span, rows, HD)
        for g in range(heads):

            @pl.when(h == g)
            def _():
                for i in range(span - 1, 0, -1):
                    reply(g, k + i, rrecv[g]).start()

                @pl.when(k > 0)
                def _():
                    reply(g, k, rrecv[g]).start()

                @pl.when(k == 0)
                def _():
                    rrecv[g][0] = rsend[g, 0]

        @pl.when(jnp.int32(k) == 0)
        def _():
            queries = recv[h, :, pl.ds(0, rows)].reshape(GROUP * rows, HD)
            grads = recv[h, :, pl.ds(rows, rows)].reshape(GROUP * rows, HD)
            score_parts = jnp.concatenate([low_grads[i] for i in range(blocks)], axis=1)
            prob_parts = jnp.concatenate([low_probs[i] for i in range(blocks)], axis=1)
            key_part = lax.dot_general(score_parts, queries, plain, preferred_element_type=jnp.float32) * scale
            value_part = lax.dot_general(prob_parts, grads, plain, preferred_element_type=jnp.float32)
            egrad[h, 0] = key_part.astype(jnp.bfloat16).reshape(stored, keys, HD)
            egrad[h, 1] = value_part.astype(jnp.bfloat16).reshape(stored, keys, HD)
            egrad_store(h).start()

    for copy in id_copies:
        copy.wait_send()
    for k in SLOTS:
        tile_copy(k).wait_send()
    for h in range(heads):
        pl.when(has_before)(shifts[h].wait_send)
        for k in SLOTS:
            request(h, k).wait_send()
    backs, out_stores = [], []
    for h in range(heads):
        if h:
            egrad_store(h - 1).wait()
            for k in SLOTS:
                reply(h - 1, k, rrecv[h - 1]).wait_send()
        for k in SLOTS:
            reply(h, k, rrecv[h]).wait_recv()
        out[h][GROUP - 1] = rrecv[h][slot_of[GROUP - 1]]
        copy = pltpu.make_async_remote_copy(
            out[h].at[GROUP - 1], oq_ref.at[0, :, columns(h)], bk_send.at[h], bk_recv.at[h],
            device_id=(s + 1, t, c), device_id_type=MESH)
        pl.when(has_after)(copy.start)
        backs.append(copy)
        for j in range(GROUP - 1):
            out[h][j] = rrecv[h][slot_of[j]]
        store = pltpu.make_async_copy(
            out[h].at[pl.ds(0, GROUP - 1)], oq_ref.at[pl.ds(1, GROUP - 1), :, columns(h)], osem.at[h])
        store.start()
        out_stores.append(store)

    for k in SLOTS:
        reply(heads - 1, k, rrecv[heads - 1]).wait_send()

    @pl.when(jnp.logical_not(has_before))
    def _():
        for h in range(heads):
            first[h] = jnp.zeros(first.shape[1:], first.dtype)
            zero = pltpu.make_async_copy(first.at[h, pl.ds(0, rows)], oq_ref.at[0, :, columns(h)], fsem.at[h, 0])
            zero.start()
            zero.wait()

    egrad_store(heads - 1).wait()
    for h in range(heads):
        out_stores[h].wait()
        pl.when(has_after)(backs[h].wait_send)
    for h in range(heads):
        pl.when(has_before)(backs[h].wait_recv)


def finish(q_in, e_in, q_out, e_out, sems):
    copies = []
    for i, (source, target) in enumerate(((q_in, q_out), (e_in.at[0], e_out.at[0]), (e_in.at[1], e_out.at[1]))):
        copy = pltpu.make_async_copy(source, target, sems.at[i])
        copy.start()
        copies.append(copy)
    for copy in copies:
        copy.wait()


def body(queries, cotangent, encoded, neighbours):
    width = queries.shape[1]
    heads = width // HD
    rows = queries.shape[0] // GROUP
    stored, keys = encoded.shape[1], encoded.shape[2]
    members = lax.axis_size("tensor") * lax.axis_size("group")
    bf16 = jnp.bfloat16
    both = 2 * rows
    dma = pltpu.SemaphoreType.DMA
    scratch = (
        [pltpu.VMEM((GROUP, both, HD), bf16) for _ in range(heads)]
        + [pltpu.VMEM((GROUP, rows, HD), bf16) for _ in range(2 * heads)]
        + [
            pltpu.VMEM((heads, GROUP, both, HD), bf16),
            pltpu.VMEM((heads, GROUP, both, HD), bf16),
            pltpu.VMEM((heads, GROUP, rows, HD), bf16),
            pltpu.VMEM((heads, both, HD), bf16),
            pltpu.VMEM((heads, 2, stored, keys, HD), bf16),
            pltpu.VMEM((heads, 2, stored, keys, HD), bf16),
            pltpu.VMEM((2, stored * keys, GROUP // 2 * rows), bf16),
            pltpu.VMEM((2, stored * keys, GROUP // 2 * rows), bf16),
            pltpu.VMEM((heads, HD, stored * keys), bf16),
            pltpu.VMEM((GROUP, 8, HD), jnp.float32),
            pltpu.VMEM((GROUP, 8, HD), jnp.float32),
            pltpu.VMEM((GROUP // 2, stored, 8, HD), jnp.float32),
            pltpu.SMEM((1, 2), jnp.int32),
            pltpu.SMEM((GROUP, 128), jnp.int32),
            dma((heads, 2)), dma((heads, 2)), dma((heads,)), dma, dma((heads,)), dma((heads,)),
            dma((members,)), dma((members,)), dma((GROUP,)), dma((GROUP,)), dma((heads,)), dma((heads,)),
            dma((heads, GROUP)), dma((heads, GROUP)), dma((heads, GROUP)), dma((heads, GROUP)),
            dma((heads,)), dma((heads,)), pltpu.SemaphoreType.REGULAR,
        ]
    )
    hbm = pl.BlockSpec(memory_space=pltpu.HBM)
    anywhere = pl.BlockSpec(memory_space=pl.ANY)
    query_grad, encoded_grad = pl.pallas_call(
        functools.partial(kernel, heads, rows, stored, keys),
        out_shape=(
            jax.ShapeDtypeStruct((GROUP, rows, width), bf16),
            jax.ShapeDtypeStruct(encoded.shape, bf16),
        ),
        in_specs=[hbm] * 4,
        out_specs=(anywhere, anywhere),
        scratch_shapes=scratch,
        compiler_params=pltpu.CompilerParams(
            collective_id=0, has_side_effects=True, vmem_limit_bytes=48 * 2**20
        ),
        cost_estimate=pl.CostEstimate(flops=10**9, bytes_accessed=3 * 2**20, transcendentals=10**6),
        name="retrieval_grads",
    )(*[
        pltpu.with_memory_space_constraint(operand, pltpu.HBM)
        for operand in (queries.reshape(GROUP, rows, width), cotangent.reshape(GROUP, rows, width), encoded, neighbours)
    ])
    query_grad, encoded_grad = pl.pallas_call(
        finish,
        out_shape=(
            pltpu.HBM((GROUP, rows, width), bf16),
            pltpu.HBM(encoded.shape, bf16),
        ),
        in_specs=[anywhere] * 2,
        out_specs=(anywhere, anywhere),
        scratch_shapes=[dma((3,))],
        compiler_params=pltpu.CompilerParams(vmem_limit_bytes=2**20),
        cost_estimate=pl.CostEstimate(flops=0, bytes_accessed=3 * 2**20, transcendentals=0),
        name="retrieval_finish",
    )(query_grad, encoded_grad)
    return query_grad.reshape(queries.shape), encoded_grad


def solution(mesh):
    placed = (
        P("seq", ("tensor", "group")),
        P("seq", ("tensor", "group")),
        P(None, "seq", None, ("tensor", "group")),
        P(("seq", "tensor", "group"), None),
    )
    return jax.shard_map(
        body,
        mesh=mesh,
        in_specs=placed,
        out_specs=(P("seq", ("tensor", "group")), P(None, "seq", None, ("tensor", "group"))),
        check_vma=False,
    )
```

```python
import functools
import math

import jax
import jax.numpy as jnp
from jax import lax
from jax.experimental import pallas as pl
from jax.experimental.pallas import tpu as pltpu
from jax.sharding import PartitionSpec as P

HD = 128
GROUP = 8
SLOTS = (6, 7, 5, 4, 2, 3, 1)
OTHERS = (2, 1, 3, 4, 6, 5, 7)
MESH = pl.DeviceIdType.MESH


def kernel(heads, rows, stored, keys, q_ref, g_ref, e_ref, n_ref, oq_ref, oe_ref, *scratch):
    x = scratch[:heads]
    rrecv = scratch[heads:2 * heads]
    out = scratch[2 * heads:3 * heads]
    (send, recv, rsend, first, enc, egrad, low_probs, low_grads, turned, tiles, gone_tiles, bias, ids, codes, fsem, xsem, esem,
     isem, osem, gsem, id_send, id_recv, tl_send, tl_recv, sh_send, sh_recv, rq_send, rq_recv, rp_send, rp_recv, bk_send,
     bk_recv, ready) = scratch[3 * heads:]
    both = 2 * rows
    width = 2 * rows
    pairs = GROUP // 2
    s = lax.axis_index("seq")
    t = lax.axis_index("tensor")
    c = lax.axis_index("group")
    count = lax.axis_size("seq")
    tensors = lax.axis_size("tensor")
    groups = lax.axis_size("group")
    members = tensors * groups
    place = lax.rem(s, GROUP)
    base = s - place
    member = t * groups + c
    has_before, has_after = s > 0, s < count - 1

    def owner_device(k):
        return (base + jnp.bitwise_xor(place, k), t, c)

    def member_device(d):
        other = jnp.bitwise_xor(member, d)
        return (s, other // groups, lax.rem(other, groups))

    barrier = pltpu.get_barrier_semaphore()
    for d in range(1, members):
        pl.semaphore_signal(barrier, inc=1, device_id=member_device(d), device_id_type=MESH)

    @pl.when(jnp.logical_and(has_before, place != 1))
    def _():
        pl.semaphore_signal(barrier, inc=1, device_id=(s - 1, t, c), device_id_type=MESH)

    @pl.when(has_after)
    def _():
        pl.semaphore_signal(barrier, inc=1, device_id=(s + 1, t, c), device_id_type=MESH)

    for k in SLOTS:

        @pl.when(place != k)
        def _():
            pl.semaphore_signal(barrier, inc=1, device_id=owner_device(k), device_id_type=MESH)

    def columns(h):
        return pl.ds(h * HD, HD)

    id_load = pltpu.make_async_copy(n_ref, ids, isem)
    id_load.start()
    first_loads, x_loads, enc_loads = [], [], []
    for h in range(heads):
        first_loads.append([
            pltpu.make_async_copy(ref.at[0, :, columns(h)], first.at[h, pl.ds(half * rows, rows)], fsem.at[h, half])
            for half, ref in enumerate((q_ref, g_ref))
        ])
        for load in first_loads[h]:
            load.start()
    for h in range(heads):
        enc_loads.append(pltpu.make_async_copy(e_ref.at[:, :, :, columns(h)], enc.at[h], esem.at[h]))
        enc_loads[h].start()
    for h in range(heads):
        x_loads.append([
            pltpu.make_async_copy(
                ref.at[pl.ds(1, GROUP - 1), :, columns(h)],
                x[h].at[pl.ds(0, GROUP - 1), pl.ds(half * rows, rows)], xsem.at[h, half])
            for half, ref in enumerate((q_ref, g_ref))
        ])
        for load in x_loads[h]:
            load.start()

    id_load.wait()
    near, far = ids[0, 0], ids[0, 1]
    owner = near // stored
    excluded = (3 - (near - owner * stored)) - (far - owner * stored)
    codes[member, 0] = lax.rem(owner, GROUP) * 4 + excluded

    mates = jnp.where(place == 0, 0, GROUP - 1 + has_after.astype(jnp.int32))
    pl.semaphore_wait(barrier, members - 1 + has_before.astype(jnp.int32) + mates)

    @pl.when(place != 0)
    def _():
        pl.semaphore_signal(ready, inc=1, device_id=(base, t, c), device_id_type=MESH)

    id_copies = []
    for d in range(1, members):
        copy = pltpu.make_async_remote_copy(
            codes.at[member], codes.at[member], id_send.at[d], id_recv.at[d], device_id=member_device(d), device_id_type=MESH)
        copy.start()
        id_copies.append(copy)
    shifts = []
    for h in range(heads):
        for load in first_loads[h]:
            load.wait()
        copy = pltpu.make_async_remote_copy(
            first.at[h], x[h].at[GROUP - 1], sh_send.at[h], sh_recv.at[h], device_id=(s - 1, t, c), device_id_type=MESH)
        pl.when(has_before)(copy.start)
        shifts.append(copy)

    for load in enc_loads:
        load.wait()

    @pl.loop(0, heads)
    def _(h):
        turned[h] = enc[h, 0].reshape(stored * keys, HD).T

    for copy in id_copies:
        copy.wait_recv()
    code = [codes[j, 0] for j in range(GROUP)]
    slot_of = [jnp.bitwise_xor(code[j] // 4, place) for j in range(GROUP)]
    row_of, left_out = [], []
    for k in range(GROUP):
        row, gone = jnp.int32(0), jnp.int32(0)
        for j in range(GROUP):
            here = slot_of[j] == k
            row = jnp.where(here, jnp.int32(j), row)
            gone = jnp.where(here, lax.rem(code[j], 4), gone)
        row_of.append(row)
        left_out.append(gone)

    def tile_copy(k):
        return pltpu.make_async_remote_copy(
            tiles.at[k], gone_tiles.at[k], tl_send.at[k], tl_recv.at[k], device_id=owner_device(k), device_id_type=MESH)

    def request(h, k):
        return pltpu.make_async_remote_copy(
            send.at[h, k], recv.at[h, k], rq_send.at[h, k], rq_recv.at[h, k], device_id=owner_device(k), device_id_type=MESH)

    def reply(h, k, target):
        return pltpu.make_async_remote_copy(
            rsend.at[h, k], target.at[k], rp_send.at[h, k], rp_recv.at[h, k], device_id=owner_device(k), device_id_type=MESH)

    def egrad_store(h):
        start = h * HD if isinstance(h, int) else pl.multiple_of(h * HD, HD)
        return pltpu.make_async_copy(egrad.at[h], oe_ref.at[:, :, :, pl.ds(start, HD)], gsem.at[h])

    @pl.when(place == 0)
    def _():
        pl.semaphore_wait(ready, GROUP - 1)

    for k in SLOTS:
        tiles[k] = jnp.full(tiles.shape[1:], left_out[k].astype(jnp.float32), jnp.float32)
        tile_copy(k).start()
    gone_tiles[0] = jnp.full(tiles.shape[1:], left_out[0].astype(jnp.float32), jnp.float32)
    for h in range(heads):
        for load in x_loads[h]:
            load.wait()
        pl.when(has_after)(shifts[h].wait_recv)

        @pl.when(jnp.logical_not(has_after))
        def _():
            x[h][GROUP - 1] = jnp.zeros(x[h].shape[1:], x[h].dtype)

        for low, high in zip(SLOTS, OTHERS):
            k = jnp.where(c == 0, jnp.int32(low), jnp.int32(high))
            send[h, k] = x[h][jnp.where(c == 0, row_of[low], row_of[high])]
            request(h, k).start()
        recv[h, 0] = x[h][row_of[0]]

    scale = 1.0 / math.sqrt(HD)
    minor = (((1,), (1,)), ((), ()))
    plain = (((1,), (0,)), ((), ()))
    lane = lax.broadcasted_iota(jnp.int32, tiles.shape[1:], 1)
    for k in SLOTS:
        tile_copy(k).wait_recv()
    for p in range(pairs):
        gone = jnp.where(lane < rows, gone_tiles[2 * p], gone_tiles[2 * p + 1])
        for m in range(stored):
            bias[p, m] = jnp.where(gone == float(m), jnp.float32(-1e30), jnp.float32(0.0))

    blocks = 2
    span = GROUP // blocks

    @pl.loop(0, heads * blocks)
    def _(step):
        h = step // blocks if blocks > 1 else step
        p = blocks - 1 - lax.rem(step, blocks) if blocks > 1 else 0
        k = span * p
        for i in range(span - 1, -1, -1):
            if i:
                request(h, k + i).wait_recv()
            elif blocks > 1:

                @pl.when(k > 0)
                def _():
                    request(h, k).wait_recv()

        queries = recv[h, pl.ds(k, span), pl.ds(0, rows)].reshape(span * rows, HD)
        grads = recv[h, pl.ds(k, span), pl.ds(rows, rows)].reshape(span * rows, HD)
        key_rows = enc[h, 0].reshape(stored * keys, HD)
        value_rows = enc[h, 1].reshape(stored * keys, HD)
        scores = lax.dot_general(key_rows, queries, minor, preferred_element_type=jnp.float32)
        grad_probs = lax.dot_general(value_rows, grads, minor, preferred_element_type=jnp.float32)
        masks = [jnp.concatenate([bias[p * (span // 2) + i, m][0:1] for i in range(span // 2)], axis=1) for m in range(stored)]
        scores = jnp.concatenate([scores[m * keys:(m + 1) * keys] * scale + masks[m] for m in range(stored)], axis=0)
        scores = jnp.exp(scores - jnp.max(scores, axis=0, keepdims=True))
        probs = scores * (1.0 / jnp.sum(scores, axis=0, keepdims=True))
        probs_low = probs.astype(jnp.bfloat16)
        delta = jnp.sum(probs_low.astype(jnp.float32) * grad_probs, axis=0, keepdims=True)
        grad_scores = (probs * (grad_probs - delta)).astype(jnp.bfloat16)
        low_probs[p] = probs_low
        low_grads[p] = grad_scores
        answer = lax.dot_general(turned[h], grad_scores, plain, preferred_element_type=jnp.float32) * scale
        rsend[h, pl.ds(k, span)] = answer.T.astype(jnp.bfloat16).reshape(span, rows, HD)
        for g in range(heads):

            @pl.when(h == g)
            def _():
                for i in range(span - 1, 0, -1):
                    reply(g, k + i, rrecv[g]).start()

                @pl.when(k > 0)
                def _():
                    reply(g, k, rrecv[g]).start()

                @pl.when(k == 0)
                def _():
                    rrecv[g][0] = rsend[g, 0]

        @pl.when(jnp.int32(k) == 0)
        def _():
            queries = recv[h, :, pl.ds(0, rows)].reshape(GROUP * rows, HD)
            grads = recv[h, :, pl.ds(rows, rows)].reshape(GROUP * rows, HD)
            score_parts = jnp.concatenate([low_grads[i] for i in range(blocks)], axis=1)
            prob_parts = jnp.concatenate([low_probs[i] for i in range(blocks)], axis=1)
            key_part = lax.dot_general(score_parts, queries, plain, preferred_element_type=jnp.float32) * scale
            value_part = lax.dot_general(prob_parts, grads, plain, preferred_element_type=jnp.float32)
            egrad[h, 0] = key_part.astype(jnp.bfloat16).reshape(stored, keys, HD)
            egrad[h, 1] = value_part.astype(jnp.bfloat16).reshape(stored, keys, HD)
            egrad_store(h).start()

    for copy in id_copies:
        copy.wait_send()
    for k in SLOTS:
        tile_copy(k).wait_send()
    for h in range(heads):
        pl.when(has_before)(shifts[h].wait_send)
        for k in SLOTS:
            request(h, k).wait_send()
    backs, out_stores = [], []
    for h in range(heads):
        if h:
            egrad_store(h - 1).wait()
            for k in SLOTS:
                reply(h - 1, k, rrecv[h - 1]).wait_send()
        for k in SLOTS:
            reply(h, k, rrecv[h]).wait_recv()
        out[h][GROUP - 1] = rrecv[h][slot_of[GROUP - 1]]
        copy = pltpu.make_async_remote_copy(
            out[h].at[GROUP - 1], oq_ref.at[0, :, columns(h)], bk_send.at[h], bk_recv.at[h],
            device_id=(s + 1, t, c), device_id_type=MESH)
        pl.when(has_after)(copy.start)
        backs.append(copy)
        for j in range(GROUP - 1):
            out[h][j] = rrecv[h][slot_of[j]]
        store = pltpu.make_async_copy(
            out[h].at[pl.ds(0, GROUP - 1)], oq_ref.at[pl.ds(1, GROUP - 1), :, columns(h)], osem.at[h])
        store.start()
        out_stores.append(store)

    for k in SLOTS:
        reply(heads - 1, k, rrecv[heads - 1]).wait_send()

    @pl.when(jnp.logical_not(has_before))
    def _():
        for h in range(heads):
            first[h] = jnp.zeros(first.shape[1:], first.dtype)
            zero = pltpu.make_async_copy(first.at[h, pl.ds(0, rows)], oq_ref.at[0, :, columns(h)], fsem.at[h, 0])
            zero.start()
            zero.wait()

    egrad_store(heads - 1).wait()
    for h in range(heads):
        out_stores[h].wait()
        pl.when(has_after)(backs[h].wait_send)
    for h in range(heads):
        pl.when(has_before)(backs[h].wait_recv)


def finish(q_in, e_in, q_out, e_out, sems):
    copies = []
    for i, (source, target) in enumerate(((q_in, q_out), (e_in.at[0], e_out.at[0]), (e_in.at[1], e_out.at[1]))):
        copy = pltpu.make_async_copy(source, target, sems.at[i])
        copy.start()
        copies.append(copy)
    for copy in copies:
        copy.wait()


def body(queries, cotangent, encoded, neighbours):
    width = queries.shape[1]
    heads = width // HD
    rows = queries.shape[0] // GROUP
    stored, keys = encoded.shape[1], encoded.shape[2]
    members = lax.axis_size("tensor") * lax.axis_size("group")
    bf16 = jnp.bfloat16
    both = 2 * rows
    dma = pltpu.SemaphoreType.DMA
    scratch = (
        [pltpu.VMEM((GROUP, both, HD), bf16) for _ in range(heads)]
        + [pltpu.VMEM((GROUP, rows, HD), bf16) for _ in range(2 * heads)]
        + [
            pltpu.VMEM((heads, GROUP, both, HD), bf16),
            pltpu.VMEM((heads, GROUP, both, HD), bf16),
            pltpu.VMEM((heads, GROUP, rows, HD), bf16),
            pltpu.VMEM((heads, both, HD), bf16),
            pltpu.VMEM((heads, 2, stored, keys, HD), bf16),
            pltpu.VMEM((heads, 2, stored, keys, HD), bf16),
            pltpu.VMEM((2, stored * keys, GROUP // 2 * rows), bf16),
            pltpu.VMEM((2, stored * keys, GROUP // 2 * rows), bf16),
            pltpu.VMEM((heads, HD, stored * keys), bf16),
            pltpu.VMEM((GROUP, 8, HD), jnp.float32),
            pltpu.VMEM((GROUP, 8, HD), jnp.float32),
            pltpu.VMEM((GROUP // 2, stored, 8, HD), jnp.float32),
            pltpu.SMEM((1, 2), jnp.int32),
            pltpu.SMEM((GROUP, 128), jnp.int32),
            dma((heads, 2)), dma((heads, 2)), dma((heads,)), dma, dma((heads,)), dma((heads,)),
            dma((members,)), dma((members,)), dma((GROUP,)), dma((GROUP,)), dma((heads,)), dma((heads,)),
            dma((heads, GROUP)), dma((heads, GROUP)), dma((heads, GROUP)), dma((heads, GROUP)),
            dma((heads,)), dma((heads,)), pltpu.SemaphoreType.REGULAR,
        ]
    )
    hbm = pl.BlockSpec(memory_space=pltpu.HBM)
    anywhere = pl.BlockSpec(memory_space=pl.ANY)
    query_grad, encoded_grad = pl.pallas_call(
        functools.partial(kernel, heads, rows, stored, keys),
        out_shape=(
            jax.ShapeDtypeStruct((GROUP, rows, width), bf16),
            jax.ShapeDtypeStruct(encoded.shape, bf16),
        ),
        in_specs=[hbm] * 4,
        out_specs=(anywhere, anywhere),
        scratch_shapes=scratch,
        compiler_params=pltpu.CompilerParams(
            collective_id=0, has_side_effects=True, vmem_limit_bytes=48 * 2**20
        ),
        cost_estimate=pl.CostEstimate(flops=10**9, bytes_accessed=3 * 2**20, transcendentals=10**6),
        name="retrieval_grads",
    )(*[
        pltpu.with_memory_space_constraint(operand, pltpu.HBM)
        for operand in (queries.reshape(GROUP, rows, width), cotangent.reshape(GROUP, rows, width), encoded, neighbours)
    ])
    query_grad, encoded_grad = pl.pallas_call(
        finish,
        out_shape=(
            pltpu.HBM((GROUP, rows, width), bf16),
            pltpu.HBM(encoded.shape, bf16),
        ),
        in_specs=[anywhere] * 2,
        out_specs=(anywhere, anywhere),
        scratch_shapes=[dma((3,))],
        compiler_params=pltpu.CompilerParams(vmem_limit_bytes=2**20),
        cost_estimate=pl.CostEstimate(flops=0, bytes_accessed=3 * 2**20, transcendentals=0),
        name="retrieval_finish",
    )(query_grad, encoded_grad)
    return query_grad.reshape(queries.shape), encoded_grad


def solution(mesh):
    placed = (
        P("seq", ("tensor", "group")),
        P("seq", ("tensor", "group")),
        P(None, "seq", None, ("tensor", "group")),
        P(("seq", "tensor", "group"), None),
    )
    return jax.shard_map(
        body,
        mesh=mesh,
        in_specs=placed,
        out_specs=(P("seq", ("tensor", "group")), P(None, "seq", None, ("tensor", "group"))),
        check_vma=False,
    )
```
